32 devices in a mesh: group: 2 (over y), dp: 16 (over z, x, core).
Axes of the slice: x: 2, y: 2, z: 4, core: 2. Of those that a mesh axis runs over, the one named last changes fastest.
Arguments:
- queries: bfloat16 [8192, 4096], P(('group', 'dp')), parts along dimension 0, may hold values from -1024 to 1024
- keys: bfloat16 [8192, 512], P(('group', 'dp')), parts along dimension 0, may hold values from -8 to 8
- values: bfloat16 [8192, 512], P(('group', 'dp')), parts along dimension 0, may hold values from -6 to 6
- out_grad: bfloat16 [8192, 4096], P(('group', 'dp')), parts along dimension 0, may hold values from -6 to 6
- branch_ids: int32 [32, 256], P(('group', 'dp')), parts along dimension 0, may hold values from 0 to 3, never falling along the last dimension, each value on 1 to 128 neighbouring positions
- node_use: int32 [32, 4, 4], P(('group', 'dp')), parts along dimension 0, may hold values 0 or 1
Outputs:
- query_grad: bfloat16 [8192, 4096], P(('group', 'dp')), parts along dimension 0
- key_grad: bfloat16 [8192, 512], P(('group', 'dp')), parts along dimension 0
- value_grad: bfloat16 [8192, 512], P(('group', 'dp')), parts along dimension 0
The draws below stay inside these ranges and needn't reach their ends.
There are 2 independent parts, one for each index of `group`. The reference program is written for one: setup_inputs(seed, part) draws one part's arguments, and reference() takes and returns one part's arrays. A program takes and returns all parts, laid end to end along the dimension named above; each array names one. Nothing has to cross between parts.
All inputs are finite; a program needn't handle non-finite values. No bound on the sum of `node_use` on one device may be relied on, other than what follows from the above.
Results may differ from the reference program's by a relative error of at most 0.015.
Values may be sent and summed in bfloat16 or wider, within the bound.
A program may use at most 192 MiB of HBM per device.

```python
import math
import jax
import jax.numpy as jnp
import numpy as np
from jax import lax

H = 32
KVH = 4
HD = 128
NODE_LEN = 128
REACH = 4
SEGS = 4
TOK_DEV = 256
OWNERS = 16
TOKENS = 4096
N_DP = 16


def shared_draw(key):
    key_rows = jnp.clip(jax.random.normal(jax.random.fold_in(key, 11), (TOKENS, KVH * HD), jnp.float32), -6.0, 6.0)
    query_rows = jnp.clip(jax.random.normal(jax.random.fold_in(key, 12), (TOKENS, H * HD), jnp.float32), -6.0, 6.0)
    return (query_rows, key_rows)


def draw_queries(key, part):
    return shared_draw(key)[0].astype(jnp.bfloat16)


def draw_keys(key, part):
    return shared_draw(key)[1].astype(jnp.bfloat16)


def with_ends(array, stream_key, low, top_value):
    index_at = [jax.random.randint(jax.random.fold_in(stream_key, axis), (), 0, length) for axis, length in enumerate(array.shape)]
    main_axis = array.shape.index(max(array.shape))
    beside = index_at[:main_axis] + [(index_at[main_axis] + 1) % array.shape[main_axis]] + index_at[main_axis + 1:]
    return array.at[tuple(index_at)].set(low).at[tuple(beside)].set(top_value)


def shard_levels(rng, extent, split, least, largest):
    loudness, own = 1.0, jax.random.fold_in(rng, 6)
    for axis_at, parts in split:
        draws = jnp.exp(jax.random.uniform(jax.random.fold_in(own, axis_at), (parts,), jnp.float32, least / len(split), largest / len(split)))
        loudness = loudness * jnp.repeat(draws, extent[axis_at] // parts).reshape([-1 if axis == axis_at else 1 for axis in range(len(extent))])
    return loudness


def split_up(count, total, most, skew):
    portions = [(1 << 20) // math.isqrt(standing ** skew) + 1 for standing in range(2, count + 1)]
    surplus, holding = total - most - (count - 1), [1] * (count - 1)
    while surplus > 0:
        candidates = [i for i in range(count - 1) if holding[i] < most]
        pool, left = sum([portions[i] for i in candidates]), surplus
        for i in candidates:
            addition = min(most - holding[i], max(1, left * portions[i] // pool), surplus)
            holding[i] = holding[i] + addition
            surplus = surplus - addition
    return np.array([most] + holding)


def ragged_sizes(rng, number_of, total, reach, slope):
    if number_of == 2:
        one = jax.random.randint(rng, (), max(1, total - reach), min(reach, total - 1) + 1)
        return jnp.stack([one, total - one])
    sizes = jnp.asarray(split_up(number_of, total, reach, slope), jnp.int32)
    twos = (number_of - 1) // 2
    donor, sink = sizes[1:1 + 2 * twos:2], sizes[2:2 + 2 * twos:2]
    margin = jnp.minimum(donor - 1, reach - sink)
    moved = jax.random.randint(jax.random.fold_in(rng, 1), (twos,), 0, 1 << 20) % (margin + 1)
    sizes = sizes.at[1:1 + 2 * twos:2].set(donor - moved).at[2:2 + 2 * twos:2].set(sink + moved)
    return sizes[jax.random.permutation(jax.random.fold_in(rng, 2), number_of)]


def gaussian(own_key, extent, spread, limit, split=(), held_as=jnp.bfloat16):
    values = spread * jax.random.normal(own_key, extent, jnp.float32)
    if split:
        values = values * shard_levels(own_key, extent, split, -0.22, 0.18)
    return jnp.clip(values, -limit, limit).astype(held_as)


def setup_inputs(seed: int = 0, part: int = 0) -> dict:
    key_of = jax.random.split(jax.random.key(seed), 7)
    part_splits = jax.random.split(jax.random.fold_in(key_of[6], part), 7)
    queries = draw_queries(jax.random.fold_in(jax.random.fold_in(key_of[6], part), 71), part)
    keys = draw_keys(jax.random.fold_in(jax.random.fold_in(key_of[6], part), 71), part)
    values = gaussian(part_splits[2], (TOKENS, KVH * HD), 1.0, 6.0, ((0, 16),))
    out_grad = gaussian(part_splits[3], (TOKENS, H * HD), 1.0, 6.0, ((0, 16),))
    branch_ids = jax.vmap(lambda own: jnp.searchsorted(jnp.cumsum(ragged_sizes(own, SEGS, TOK_DEV, TOK_DEV // 2, 2)), jnp.arange(TOK_DEV), side="right"))(jax.random.split(part_splits[4], OWNERS)).reshape((OWNERS, TOK_DEV)).astype(jnp.int32)
    node_use = with_ends((jax.random.randint(part_splits[5], (OWNERS, SEGS, REACH), 0, 2) < 1).astype(jnp.int32), jax.random.fold_in(part_splits[5], 1), 0, 1)
    return dict(queries=queries, keys=keys, values=values, out_grad=out_grad, branch_ids=branch_ids, node_use=node_use)


def device_backward(query_blk, key_all, value_all, grad_blk, branch_row, use_table):
    tok_count = query_blk.shape[0]
    key_count = key_all.shape[0]
    groups = H // KVH
    scale = 1.0 / (HD ** 0.5)
    query_four = query_blk.reshape(tok_count, KVH, groups, HD).astype(jnp.float32)
    grad_four = grad_blk.reshape(tok_count, KVH, groups, HD).astype(jnp.float32)
    key_three = key_all.reshape(key_count, KVH, HD).astype(jnp.float32)
    value_three = value_all.reshape(key_count, KVH, HD).astype(jnp.float32)
    position = jnp.arange(tok_count)
    local_mask = (branch_row[:, None] == branch_row[None, :]) & (position[None, :] <= position[:, None])
    node_flags = use_table[branch_row] > 0
    node_mask = jnp.repeat(node_flags, NODE_LEN, axis=1)
    visible = jnp.concatenate([local_mask, node_mask], axis=1)
    scores = jnp.einsum('tkgd,skd->kgts', query_four, key_three) * scale
    scores = jnp.where(visible[None, None], scores, -jnp.inf)
    norm_log = jax.nn.logsumexp(scores, axis=-1, keepdims=True)
    weights = jnp.exp(scores - norm_log)
    weight_low = weights.astype(jnp.bfloat16).astype(jnp.float32)
    value_terms = jnp.einsum('kgts,tkgd->skd', weight_low, grad_four)
    dprob = jnp.einsum('tkgd,skd->kgts', grad_four, value_three)
    delta = jnp.sum(weights * dprob, axis=-1, keepdims=True)
    dscore = (weights * (dprob - delta)).astype(jnp.bfloat16).astype(jnp.float32)
    query_grad = (jnp.einsum('kgts,skd->tkgd', dscore, key_three) * scale).astype(jnp.bfloat16)
    key_terms = jnp.einsum('kgts,tkgd->skd', dscore, query_four) * scale
    return (query_grad.reshape(tok_count, H * HD), key_terms.reshape(key_count, KVH * HD),
            value_terms.reshape(key_count, KVH * HD))


def reference(queries, keys, values, out_grad, branch_ids, node_use):
    owners = N_DP
    width = KVH * HD
    query_blocks = queries.reshape(owners, TOK_DEV, H * HD)
    grad_blocks = out_grad.reshape(owners, TOK_DEV, H * HD)
    key_blocks = keys.reshape(owners, TOK_DEV, width)
    value_blocks = values.reshape(owners, TOK_DEV, width)
    node_keys = key_blocks[:, :NODE_LEN]
    node_values = value_blocks[:, :NODE_LEN]

    def one_device(device):
        source = (device - jnp.arange(1, REACH + 1)) % owners
        key_all = jnp.concatenate([key_blocks[device], node_keys[source].reshape(REACH * NODE_LEN, width)], axis=0)
        value_all = jnp.concatenate([value_blocks[device], node_values[source].reshape(REACH * NODE_LEN, width)], axis=0)
        return device_backward(query_blocks[device], key_all, value_all, grad_blocks[device],
                               branch_ids[device], node_use[device])

    query_grad, key_terms, value_terms = lax.map(one_device, jnp.arange(owners))
    key_total = key_terms[:, :TOK_DEV]
    value_total = value_terms[:, :TOK_DEV]
    key_nodes = key_terms[:, TOK_DEV:].reshape(owners, REACH, NODE_LEN, width)
    value_nodes = value_terms[:, TOK_DEV:].reshape(owners, REACH, NODE_LEN, width)
    for offset in range(REACH):
        key_total = key_total.at[:, :NODE_LEN].add(jnp.roll(key_nodes[:, offset], -(offset + 1), axis=0))
        value_total = value_total.at[:, :NODE_LEN].add(jnp.roll(value_nodes[:, offset], -(offset + 1), axis=0))
    return (query_grad.reshape(TOKENS, H * HD),
            key_total.reshape(TOKENS, width).astype(jnp.bfloat16),
            value_total.reshape(TOKENS, width).astype(jnp.bfloat16))
```

```python
import math

import jax
import jax.numpy as jnp
from jax import lax
from jax.experimental import pallas as pl
from jax.experimental.pallas import tpu as pltpu
from jax.sharding import PartitionSpec as P

H = 32
KVH = 4
HD = 128
NODE_LEN = 128
REACH = 4
SEGS = 4
GROUPS = H // KVH
UNROLL = 2
HIDDEN = -1e30
MESH = pl.DeviceIdType.MESH


def fill_bias(branch_ref, use_ref, bias):
    tok = branch_ref.shape[1]
    row = branch_ref[...]
    key_branch = jnp.broadcast_to(row.astype(jnp.float32), (tok, tok)).T
    query_branch = jnp.broadcast_to(row.astype(jnp.float32), (tok, tok))
    key_at = lax.broadcasted_iota(jnp.int32, (tok, tok), 0)
    query_at = lax.broadcasted_iota(jnp.int32, (tok, tok), 1)
    local = (key_branch == query_branch) & (key_at <= query_at)
    bias[0:tok, :] = jnp.where(local, 0.0, HIDDEN)
    for r in range(REACH):
        flag = jnp.zeros((1, tok), jnp.int32)
        for slot in range(SEGS):
            flag = jnp.where(row == slot, use_ref[0, slot, r], flag)
        line = jnp.where(flag > 0, 0.0, HIDDEN).astype(jnp.float32)
        bias[tok + r * NODE_LEN : tok + (r + 1) * NODE_LEN, :] = jnp.broadcast_to(
            line, (NODE_LEN, tok)
        )


def kernel(
    q_hbm, k_hbm, v_hbm, g_hbm, branch_ref, use_ref,
    dq_hbm, dk_hbm, dv_hbm,
    q_s, g_s, dq_s, k_s, v_s, dk_s, dv_s, bias, back_out, back_in, dk_o, dv_o,
    in_sem, out_sem, k_send, k_recv, v_send, v_recv, back_send, back_recv,
):
    count = lax.axis_size("dp")
    me = lax.axis_index("dp")
    group = lax.axis_index("group")
    tok = q_hbm.shape[0]
    wide = GROUPS * HD
    scale = 1.0 / HD**0.5
    scale2 = scale * math.log2(math.e)

    def ahead(steps):
        return (group, lax.rem(me + steps + count, count))

    def cols(a, width):
        return pl.ds(pl.multiple_of(a * width, width), width)

    def load(a, which):
        if which < 2:
            source, target = ((q_hbm, q_s), (g_hbm, g_s))[which]
            return pltpu.make_async_copy(
                source.at[:, cols(a, wide)], target.at[:, cols(a, wide)], in_sem.at[which, a]
            )
        source, target = ((k_hbm, k_s), (v_hbm, v_s))[which - 2]
        return pltpu.make_async_copy(
            source.at[:, cols(a, HD)], target.at[a, pl.ds(0, tok)], in_sem.at[which, a]
        )

    def forward(a, r, which):
        source, target, send, recv = (
            (k_hbm, k_s, k_send, k_recv),
            (v_hbm, v_s, v_send, v_recv),
        )[which]
        return pltpu.make_async_remote_copy(
            src_ref=source.at[pl.ds(0, NODE_LEN), cols(a, HD)],
            dst_ref=target.at[a, pl.ds(tok + r * NODE_LEN, NODE_LEN)],
            send_sem=send.at[a, r],
            recv_sem=recv.at[a, r],
            device_id=ahead(r + 1),
            device_id_type=MESH,
        )

    def back(a, r):
        return pltpu.make_async_remote_copy(
            src_ref=back_out.at[a, r],
            dst_ref=back_in.at[a, r],
            send_sem=back_send.at[a, r],
            recv_sem=back_recv.at[a, r],
            device_id=ahead(-(r + 1)),
            device_id_type=MESH,
        )

    def store_query(a):
        return pltpu.make_async_copy(
            dq_s.at[:, cols(a, wide)], dq_hbm.at[:, cols(a, wide)], out_sem.at[a]
        )

    @pl.loop(0, KVH)
    def _(a):
        for which in range(4):
            load(a, which).start()

    barrier = pltpu.get_barrier_semaphore()
    for r in range(REACH):
        for side in (r + 1, -(r + 1)):
            pl.semaphore_signal(barrier, inc=1, device_id=ahead(side), device_id_type=MESH)
    pl.semaphore_wait(barrier, 2 * REACH)

    @pl.loop(0, KVH)
    def _(a):
        for r in range(REACH):
            for which in range(2):
                forward(a, r, which).start()

    fill_bias(branch_ref, use_ref, bias)

    @pl.loop(0, KVH)
    def _(a):
        for which in range(4):
            load(a, which).wait()
        for r in range(REACH):
            for which in range(2):
                forward(a, r, which).wait()
        dk_s[a] = jnp.zeros(dk_s.shape[1:], jnp.float32)
        dv_s[a] = jnp.zeros(dv_s.shape[1:], jnp.float32)
        key = k_s[a]
        value = v_s[a]
        key_turned = key.T

        def one_head(b):
            at = cols(a * GROUPS + b, HD)
            query = q_s[:, at]
            grad = g_s[:, at]
            scores = lax.dot_general(
                key, query, (((1,), (1,)), ((), ())), preferred_element_type=jnp.float32
            )
            scores = scores * scale2 + bias[...]
            dprob = lax.dot_general(
                value, grad, (((1,), (1,)), ((), ())), preferred_element_type=jnp.float32
            )
            top = jnp.max(scores, axis=0, keepdims=True)
            power = jnp.exp2(scores - top)
            total = jnp.sum(power, axis=0, keepdims=True)
            share = 1.0 / total
            delta = jnp.sum(power * dprob, axis=0, keepdims=True) * share
            weights = power * share
            dscore = (weights * (dprob - delta)).astype(jnp.bfloat16)
            dv = jnp.dot(weights.astype(jnp.bfloat16), grad, preferred_element_type=jnp.float32)
            dk = jnp.dot(dscore, query, preferred_element_type=jnp.float32)
            dq = jnp.dot(key_turned, dscore, preferred_element_type=jnp.float32)
            dq_s[:, at] = (dq * scale).T.astype(jnp.bfloat16)
            return dk, dv

        @pl.loop(0, GROUPS // UNROLL)
        def _(pair):
            parts = [one_head(pair * UNROLL + i) for i in range(UNROLL)]
            dk, dv = parts[0]
            for more in parts[1:]:
                dk = dk + more[0]
                dv = dv + more[1]
            dk_s[a] += dk
            dv_s[a] += dv

        for r in range(REACH):
            rows = pl.ds(tok + r * NODE_LEN, NODE_LEN)
            back_out[a, r, 0] = (dk_s[a, rows] * scale).astype(jnp.bfloat16)
            back_out[a, r, 1] = dv_s[a, rows].astype(jnp.bfloat16)
            back(a, r).start()
        store_query(a).start()

    for a in range(KVH):
        at = slice(a * HD, (a + 1) * HD)
        dk = dk_s[a, 0:tok] * scale
        dv = dv_s[a, 0:tok]
        dk_o[NODE_LEN:tok, at] = dk[NODE_LEN:].astype(jnp.bfloat16)
        dv_o[NODE_LEN:tok, at] = dv[NODE_LEN:].astype(jnp.bfloat16)
        dk, dv = dk[:NODE_LEN], dv[:NODE_LEN]
        for r in range(REACH):
            back(a, r).wait()
            dk = dk + back_in[a, r, 0].astype(jnp.float32)
            dv = dv + back_in[a, r, 1].astype(jnp.float32)
        dk_o[0:NODE_LEN, at] = dk.astype(jnp.bfloat16)
        dv_o[0:NODE_LEN, at] = dv.astype(jnp.bfloat16)
    last_k = pltpu.make_async_copy(dk_o, dk_hbm, out_sem.at[KVH])
    last_v = pltpu.make_async_copy(dv_o, dv_hbm, out_sem.at[KVH + 1])
    last_k.start()
    last_v.start()
    for a in range(KVH):
        store_query(a).wait()
    last_k.wait()
    last_v.wait()


def shards(queries, keys, values, out_grad, branch_ids, node_use):
    tok = queries.shape[0]
    every = tok + REACH * NODE_LEN
    low = jnp.bfloat16
    dma = pltpu.SemaphoreType.DMA
    anywhere = pl.BlockSpec(memory_space=pl.ANY)
    flops = 5 * 2 * tok * every * H * HD
    return pl.pallas_call(
        kernel,
        out_shape=(
            jax.ShapeDtypeStruct(queries.shape, low),
            jax.ShapeDtypeStruct(keys.shape, low),
            jax.ShapeDtypeStruct(values.shape, low),
        ),
        in_specs=[anywhere] * 4
        + [pl.BlockSpec(memory_space=pltpu.VMEM), pl.BlockSpec(memory_space=pltpu.SMEM)],
        out_specs=(anywhere,) * 3,
        scratch_shapes=[
            pltpu.VMEM((tok, H * HD), low),
            pltpu.VMEM((tok, H * HD), low),
            pltpu.VMEM((tok, H * HD), low),
            pltpu.VMEM((KVH, every, HD), low),
            pltpu.VMEM((KVH, every, HD), low),
            pltpu.VMEM((KVH, every, HD), jnp.float32),
            pltpu.VMEM((KVH, every, HD), jnp.float32),
            pltpu.VMEM((every, tok), jnp.float32),
            pltpu.VMEM((KVH, REACH, 2, NODE_LEN, HD), low),
            pltpu.VMEM((KVH, REACH, 2, NODE_LEN, HD), low),
            pltpu.VMEM((tok, KVH * HD), low),
            pltpu.VMEM((tok, KVH * HD), low),
            dma((4, KVH)),
            dma((KVH + 2,)),
            dma((KVH, REACH)),
            dma((KVH, REACH)),
            dma((KVH, REACH)),
            dma((KVH, REACH)),
            dma((KVH, REACH)),
            dma((KVH, REACH)),
        ],
        compiler_params=pltpu.CompilerParams(
            collective_id=0, has_side_effects=True, vmem_limit_bytes=48 * 1024 * 1024
        ),
        cost_estimate=pl.CostEstimate(
            flops=flops, bytes_accessed=8 * 1024 * 1024, transcendentals=tok * every * H
        ),
    )(queries, keys, values, out_grad, branch_ids, node_use)


def solution(mesh):
    rows = P(("group", "dp"), None)
    return jax.shard_map(
        shards,
        mesh=mesh,
        in_specs=(rows, rows, rows, rows, rows, P(("group", "dp"), None, None)),
        out_specs=(rows, rows, rows),
        check_vma=False,
    )
```

```python
import math

import jax
import jax.numpy as jnp
from jax import lax
from jax.experimental import pallas as pl
from jax.experimental.pallas import tpu as pltpu
from jax.sharding import PartitionSpec as P

H = 32
KVH = 4
HD = 128
NODE_LEN = 128
REACH = 4
SEGS = 4
GROUPS = H // KVH
UNROLL = 8
HIDDEN = -1e30
MESH = pl.DeviceIdType.MESH


def fill_bias(branch_ref, use_ref, bias):
    tok = branch_ref.shape[1]
    row = branch_ref[...]
    key_branch = jnp.broadcast_to(row.astype(jnp.float32), (tok, tok)).T
    query_branch = jnp.broadcast_to(row.astype(jnp.float32), (tok, tok))
    key_at = lax.broadcasted_iota(jnp.int32, (tok, tok), 0)
    query_at = lax.broadcasted_iota(jnp.int32, (tok, tok), 1)
    local = (key_branch == query_branch) & (key_at <= query_at)
    bias[0:tok, :] = jnp.where(local, 0.0, HIDDEN)
    for r in range(REACH):
        flag = jnp.zeros((1, tok), jnp.int32)
        for slot in range(SEGS):
            flag = jnp.where(row == slot, use_ref[0, slot, r], flag)
        line = jnp.where(flag > 0, 0.0, HIDDEN).astype(jnp.float32)
        bias[tok + r * NODE_LEN : tok + (r + 1) * NODE_LEN, :] = jnp.broadcast_to(
            line, (NODE_LEN, tok)
        )


def kernel(
    q_hbm, k_hbm, v_hbm, g_hbm, branch_ref, use_ref,
    dq_hbm, dk_hbm, dv_hbm,
    q_s, g_s, dq_s, k_s, v_s, dk_s, dv_s, bias, back_out, back_in, dk_o, dv_o,
    in_sem, out_sem, k_send, k_recv, v_send, v_recv, back_send, back_recv,
):
    count = lax.axis_size("dp")
    me = lax.axis_index("dp")
    group = lax.axis_index("group")
    tok = q_hbm.shape[0]
    wide = GROUPS * HD
    scale = 1.0 / HD**0.5
    scale2 = scale * math.log2(math.e)

    def ahead(steps):
        return (group, lax.rem(me + steps + count, count))

    def cols(a, width):
        return pl.ds(pl.multiple_of(a * width, width), width)

    def load(a, which):
        if which < 2:
            source, target = ((q_hbm, q_s), (g_hbm, g_s))[which]
            return pltpu.make_async_copy(
                source.at[:, cols(a, wide)], target.at[:, cols(a, wide)], in_sem.at[which, a]
            )
        source, target = ((k_hbm, k_s), (v_hbm, v_s))[which - 2]
        return pltpu.make_async_copy(
            source.at[:, cols(a, HD)], target.at[a, pl.ds(0, tok)], in_sem.at[which, a]
        )

    def forward(a, r, which):
        target, send, recv = ((k_s, k_send, k_recv), (v_s, v_send, v_recv))[which]
        return pltpu.make_async_remote_copy(
            src_ref=target.at[a, pl.ds(0, NODE_LEN)],
            dst_ref=target.at[a, pl.ds(tok + r * NODE_LEN, NODE_LEN)],
            send_sem=send.at[a, r],
            recv_sem=recv.at[a, r],
            device_id=ahead(r + 1),
            device_id_type=MESH,
        )

    def back(a, r):
        return pltpu.make_async_remote_copy(
            src_ref=back_out.at[a, r],
            dst_ref=back_in.at[a, r],
            send_sem=back_send.at[a, r],
            recv_sem=back_recv.at[a, r],
            device_id=ahead(-(r + 1)),
            device_id_type=MESH,
        )

    def store_query(a):
        return pltpu.make_async_copy(
            dq_s.at[:, cols(a, wide)], dq_hbm.at[:, cols(a, wide)], out_sem.at[a]
        )

    @pl.loop(0, KVH)
    def _(a):
        for which in (2, 3, 0, 1):
            load(a, which).start()

    barrier = pltpu.get_barrier_semaphore()
    for r in range(REACH):
        for side in (r + 1, -(r + 1)):
            pl.semaphore_signal(barrier, inc=1, device_id=ahead(side), device_id_type=MESH)
    pl.semaphore_wait(barrier, 2 * REACH)

    @pl.loop(0, KVH)
    def _(a):
        for which in range(2):
            load(a, which + 2).wait()
        for r in range(REACH):
            for which in range(2):
                forward(a, r, which).start()

    fill_bias(branch_ref, use_ref, bias)

    @pl.loop(0, KVH)
    def _(a):
        for which in range(2):
            load(a, which).wait()
        for r in range(REACH):
            for which in range(2):
                forward(a, r, which).wait()
        dk_s[a] = jnp.zeros(dk_s.shape[1:], jnp.float32)
        dv_s[a] = jnp.zeros(dv_s.shape[1:], jnp.float32)
        key = k_s[a]
        value = v_s[a]
        key_turned = key.T

        def one_head(b):
            at = cols(a * GROUPS + b, HD)
            query = q_s[:, at]
            grad = g_s[:, at]
            scores = lax.dot_general(
                key, query, (((1,), (1,)), ((), ())), preferred_element_type=jnp.float32
            )
            scores = scores * scale2 + bias[...]
            dprob = lax.dot_general(
                value, grad, (((1,), (1,)), ((), ())), preferred_element_type=jnp.float32
            )
            top = jnp.max(scores, axis=0, keepdims=True)
            power = jnp.exp2(scores - top)
            total = jnp.sum(power, axis=0, keepdims=True)
            share = 1.0 / total
            delta = jnp.sum(power * dprob, axis=0, keepdims=True) * share
            weights = power * share
            dscore = (weights * (dprob - delta)).astype(jnp.bfloat16)
            dv = jnp.dot(weights.astype(jnp.bfloat16), grad, preferred_element_type=jnp.float32)
            dk = jnp.dot(dscore, query, preferred_element_type=jnp.float32)
            dq = jnp.dot(key_turned, dscore, preferred_element_type=jnp.float32)
            dq_s[:, at] = (dq * scale).T.astype(jnp.bfloat16)
            return dk, dv

        @pl.loop(0, GROUPS // UNROLL)
        def _(pair):
            parts = [one_head(pair * UNROLL + i) for i in range(UNROLL)]
            dk, dv = parts[0]
            for more in parts[1:]:
                dk = dk + more[0]
                dv = dv + more[1]
            dk_s[a] += dk
            dv_s[a] += dv

        for r in range(REACH):
            rows = pl.ds(tok + r * NODE_LEN, NODE_LEN)
            back_out[a, r, 0] = (dk_s[a, rows] * scale).astype(jnp.bfloat16)
            back_out[a, r, 1] = dv_s[a, rows].astype(jnp.bfloat16)
            back(a, r).start()
        store_query(a).start()

    for a in range(KVH):
        at = slice(a * HD, (a + 1) * HD)
        dk = dk_s[a, 0:tok] * scale
        dv = dv_s[a, 0:tok]
        dk_o[NODE_LEN:tok, at] = dk[NODE_LEN:].astype(jnp.bfloat16)
        dv_o[NODE_LEN:tok, at] = dv[NODE_LEN:].astype(jnp.bfloat16)
        dk, dv = dk[:NODE_LEN], dv[:NODE_LEN]
        for r in range(REACH):
            back(a, r).wait()
            dk = dk + back_in[a, r, 0].astype(jnp.float32)
            dv = dv + back_in[a, r, 1].astype(jnp.float32)
        dk_o[0:NODE_LEN, at] = dk.astype(jnp.bfloat16)
        dv_o[0:NODE_LEN, at] = dv.astype(jnp.bfloat16)
    last_k = pltpu.make_async_copy(dk_o, dk_hbm, out_sem.at[KVH])
    last_v = pltpu.make_async_copy(dv_o, dv_hbm, out_sem.at[KVH + 1])
    last_k.start()
    last_v.start()
    for a in range(KVH):
        store_query(a).wait()
    last_k.wait()
    last_v.wait()


def shards(queries, keys, values, out_grad, branch_ids, node_use):
    tok = queries.shape[0]
    every = tok + REACH * NODE_LEN
    low = jnp.bfloat16
    dma = pltpu.SemaphoreType.DMA
    anywhere = pl.BlockSpec(memory_space=pl.ANY)
    flops = 5 * 2 * tok * every * H * HD
    return pl.pallas_call(
        kernel,
        out_shape=(
            jax.ShapeDtypeStruct(queries.shape, low),
            jax.ShapeDtypeStruct(keys.shape, low),
            jax.ShapeDtypeStruct(values.shape, low),
        ),
        in_specs=[anywhere] * 4
        + [pl.BlockSpec(memory_space=pltpu.VMEM), pl.BlockSpec(memory_space=pltpu.SMEM)],
        out_specs=(anywhere,) * 3,
        scratch_shapes=[
            pltpu.VMEM((tok, H * HD), low),
            pltpu.VMEM((tok, H * HD), low),
            pltpu.VMEM((tok, H * HD), low),
            pltpu.VMEM((KVH, every, HD), low),
            pltpu.VMEM((KVH, every, HD), low),
            pltpu.VMEM((KVH, every, HD), jnp.float32),
            pltpu.VMEM((KVH, every, HD), jnp.float32),
            pltpu.VMEM((every, tok), jnp.float32),
            pltpu.VMEM((KVH, REACH, 2, NODE_LEN, HD), low),
            pltpu.VMEM((KVH, REACH, 2, NODE_LEN, HD), low),
            pltpu.VMEM((tok, KVH * HD), low),
            pltpu.VMEM((tok, KVH * HD), low),
            dma((4, KVH)),
            dma((KVH + 2,)),
            dma((KVH, REACH)),
            dma((KVH, REACH)),
            dma((KVH, REACH)),
            dma((KVH, REACH)),
            dma((KVH, REACH)),
            dma((KVH, REACH)),
        ],
        compiler_params=pltpu.CompilerParams(
            collective_id=0, has_side_effects=True, vmem_limit_bytes=48 * 1024 * 1024
        ),
        cost_estimate=pl.CostEstimate(
            flops=flops, bytes_accessed=8 * 1024 * 1024, transcendentals=tok * every * H
        ),
    )(queries, keys, values, out_grad, branch_ids, node_use)


def solution(mesh):
    rows = P(("group", "dp"), None)
    return jax.shard_map(
        shards,
        mesh=mesh,
        in_specs=(rows, rows, rows, rows, rows, P(("group", "dp"), None, None)),
        out_specs=(rows, rows, rows),
        check_vma=False,
    )
```

```python
import math

import jax
import jax.numpy as jnp
from jax import lax
from jax.experimental import pallas as pl
from jax.experimental.pallas import tpu as pltpu
from jax.sharding import PartitionSpec as P

H = 32
KVH = 4
HD = 128
NODE_LEN = 128
REACH = 4
SEGS = 4
GROUPS = H // KVH
UNROLL = 8
SPAN = 1
HIDDEN = -1e30
MESH = pl.DeviceIdType.MESH


def fill_bias(branch_ref, use_ref, bias):
    tok = branch_ref.shape[1]
    row = branch_ref[...]
    key_branch = jnp.broadcast_to(row.astype(jnp.float32), (tok, tok)).T
    query_branch = jnp.broadcast_to(row.astype(jnp.float32), (tok, tok))
    key_at = lax.broadcasted_iota(jnp.int32, (tok, tok), 0)
    query_at = lax.broadcasted_iota(jnp.int32, (tok, tok), 1)
    local = (key_branch == query_branch) & (key_at <= query_at)
    bias[...] = jnp.where(local, 0.0, HIDDEN)
    lines = []
    for r in range(REACH):
        flag = jnp.zeros((1, tok), jnp.int32)
        for slot in range(SEGS):
            flag = jnp.where(row == slot, use_ref[0, slot, r], flag)
        line = jnp.where(flag > 0, 0.0, HIDDEN).astype(jnp.float32)
        lines.append(line)
    return lines


def kernel(
    q_hbm, k_hbm, v_hbm, g_hbm, branch_ref, use_ref,
    dq_hbm, dk_hbm, dv_hbm,
    q_s, g_s, dq_s, kv_s, dk_s, dv_s, bias, back_out, back_in, dk_o, dv_o,
    in_sem, out_sem, kv_send, kv_recv, back_send, back_recv,
):
    count = lax.axis_size("dp")
    me = lax.axis_index("dp")
    group = lax.axis_index("group")
    tok = q_hbm.shape[0]
    wide = GROUPS * HD
    scale = 1.0 / HD**0.5
    scale2 = scale * math.log2(math.e)

    def ahead(steps):
        return (group, lax.rem(me + steps + count, count))

    def cols(a, width):
        return pl.ds(pl.multiple_of(a * width, width), width)

    def load(a, which):
        if which < 2:
            source, target = ((q_hbm, q_s), (g_hbm, g_s))[which]
            return pltpu.make_async_copy(
                source.at[:, cols(a, wide)], target.at[:, cols(a, wide)], in_sem.at[which, a]
            )
        return pltpu.make_async_copy(
            (k_hbm, v_hbm)[which - 2].at[:, cols(a, HD)],
            kv_s.at[a, which - 2, pl.ds(0, tok)],
            in_sem.at[which, a],
        )

    def forward(part, r):
        heads = pl.ds(part * SPAN, SPAN)
        return pltpu.make_async_remote_copy(
            src_ref=kv_s.at[heads, :, pl.ds(0, NODE_LEN)],
            dst_ref=kv_s.at[heads, :, pl.ds(tok + r * NODE_LEN, NODE_LEN)],
            send_sem=kv_send.at[part, r],
            recv_sem=kv_recv.at[part, r],
            device_id=ahead(r + 1),
            device_id_type=MESH,
        )

    def back(a, r):
        return pltpu.make_async_remote_copy(
            src_ref=back_out.at[a, r],
            dst_ref=back_in.at[a, r],
            send_sem=back_send.at[a, r],
            recv_sem=back_recv.at[a, r],
            device_id=ahead(-(r + 1)),
            device_id_type=MESH,
        )

    def store_query(a):
        return pltpu.make_async_copy(
            dq_s.at[:, cols(a, wide)], dq_hbm.at[:, cols(a, wide)], out_sem.at[a]
        )

    @pl.loop(0, KVH)
    def _(a):
        for which in (2, 3, 0, 1):
            load(a, which).start()

    barrier = pltpu.get_barrier_semaphore()
    for r in range(REACH):
        for side in (r + 1, -(r + 1)):
            pl.semaphore_signal(barrier, inc=1, device_id=ahead(side), device_id_type=MESH)
    pl.semaphore_wait(barrier, 2 * REACH)

    @pl.loop(0, KVH // SPAN)
    def _(part):
        for i in range(SPAN):
            for which in range(2):
                load(part * SPAN + i, which + 2).wait()
        for r in range(REACH):
            forward(part, r).start()

    lines = fill_bias(branch_ref, use_ref, bias)

    @pl.loop(0, KVH)
    def _(a):
        for which in range(2):
            load(a, which).wait()

        @pl.when(lax.rem(a, SPAN) == 0)
        def _():
            for r in range(REACH):
                forward(a // SPAN, r).wait()

        dk_s[a] = jnp.zeros(dk_s.shape[1:], jnp.float32)
        dv_s[a] = jnp.zeros(dv_s.shape[1:], jnp.float32)
        key = kv_s[a, 0]
        value = kv_s[a, 1]
        key_turned = key.T

        def one_head(b):
            at = cols(a * GROUPS + b, HD)
            query = q_s[:, at]
            grad = g_s[:, at]
            scores = lax.dot_general(
                key, query, (((1,), (1,)), ((), ())), preferred_element_type=jnp.float32
            )
            dprob = lax.dot_general(
                value, grad, (((1,), (1,)), ((), ())), preferred_element_type=jnp.float32
            )
            local = scores[:tok] * scale2 + bias[...]
            nodes = [scores[tok + r * NODE_LEN : tok + (r + 1) * NODE_LEN] for r in range(REACH)]
            top = jnp.max(local, axis=0, keepdims=True)
            for node, line in zip(nodes, lines):
                top = jnp.maximum(top, jnp.max(node, axis=0, keepdims=True) * scale2 + line)
            power = jnp.exp2(
                jnp.concatenate(
                    [local - top]
                    + [node * scale2 + (line - top) for node, line in zip(nodes, lines)],
                    axis=0,
                )
            )
            total = jnp.sum(power, axis=0, keepdims=True)
            share = 1.0 / total
            delta = jnp.sum(power * dprob, axis=0, keepdims=True) * share
            weights = power * share
            dscore = (weights * (dprob - delta)).astype(jnp.bfloat16)
            dv = jnp.dot(weights.astype(jnp.bfloat16), grad, preferred_element_type=jnp.float32)
            dk = jnp.dot(dscore, query, preferred_element_type=jnp.float32)
            dq = jnp.dot(key_turned, dscore, preferred_element_type=jnp.float32)
            dq_s[:, at] = (dq * scale).T.astype(jnp.bfloat16)
            return dk, dv

        @pl.loop(0, GROUPS // UNROLL)
        def _(pair):
            parts = [one_head(pair * UNROLL + i) for i in range(UNROLL)]
            dk, dv = parts[0]
            for more in parts[1:]:
                dk = dk + more[0]
                dv = dv + more[1]
            dk_s[a] += dk
            dv_s[a] += dv

        for r in range(REACH):
            rows = pl.ds(tok + r * NODE_LEN, NODE_LEN)
            back_out[a, r, 0] = (dk_s[a, rows] * scale).astype(jnp.bfloat16)
            back_out[a, r, 1] = dv_s[a, rows].astype(jnp.bfloat16)
            back(a, r).start()
        store_query(a).start()

    for a in range(KVH):
        at = slice(a * HD, (a + 1) * HD)
        dk = dk_s[a, 0:tok] * scale
        dv = dv_s[a, 0:tok]
        dk_o[NODE_LEN:tok, at] = dk[NODE_LEN:].astype(jnp.bfloat16)
        dv_o[NODE_LEN:tok, at] = dv[NODE_LEN:].astype(jnp.bfloat16)
        dk, dv = dk[:NODE_LEN], dv[:NODE_LEN]
        for r in range(REACH):
            back(a, r).wait()
            dk = dk + back_in[a, r, 0].astype(jnp.float32)
            dv = dv + back_in[a, r, 1].astype(jnp.float32)
        dk_o[0:NODE_LEN, at] = dk.astype(jnp.bfloat16)
        dv_o[0:NODE_LEN, at] = dv.astype(jnp.bfloat16)
    last_k = pltpu.make_async_copy(dk_o, dk_hbm, out_sem.at[KVH])
    last_v = pltpu.make_async_copy(dv_o, dv_hbm, out_sem.at[KVH + 1])
    last_k.start()
    last_v.start()
    for a in range(KVH):
        store_query(a).wait()
    last_k.wait()
    last_v.wait()


def shards(queries, keys, values, out_grad, branch_ids, node_use):
    tok = queries.shape[0]
    every = tok + REACH * NODE_LEN
    low = jnp.bfloat16
    dma = pltpu.SemaphoreType.DMA
    anywhere = pl.BlockSpec(memory_space=pl.ANY)
    flops = 5 * 2 * tok * every * H * HD
    return pl.pallas_call(
        kernel,
        out_shape=(
            jax.ShapeDtypeStruct(queries.shape, low),
            jax.ShapeDtypeStruct(keys.shape, low),
            jax.ShapeDtypeStruct(values.shape, low),
        ),
        in_specs=[anywhere] * 4
        + [pl.BlockSpec(memory_space=pltpu.VMEM), pl.BlockSpec(memory_space=pltpu.SMEM)],
        out_specs=(anywhere,) * 3,
        scratch_shapes=[
            pltpu.VMEM((tok, H * HD), low),
            pltpu.VMEM((tok, H * HD), low),
            pltpu.VMEM((tok, H * HD), low),
            pltpu.VMEM((KVH, 2, every, HD), low),
            pltpu.VMEM((KVH, every, HD), jnp.float32),
            pltpu.VMEM((KVH, every, HD), jnp.float32),
            pltpu.VMEM((tok, tok), jnp.float32),
            pltpu.VMEM((KVH, REACH, 2, NODE_LEN, HD), low),
            pltpu.VMEM((KVH, REACH, 2, NODE_LEN, HD), low),
            pltpu.VMEM((tok, KVH * HD), low),
            pltpu.VMEM((tok, KVH * HD), low),
            dma((4, KVH)),
            dma((KVH + 2,)),
            dma((KVH // SPAN, REACH)),
            dma((KVH // SPAN, REACH)),
            dma((KVH, REACH)),
            dma((KVH, REACH)),
        ],
        compiler_params=pltpu.CompilerParams(
            collective_id=0, has_side_effects=True, vmem_limit_bytes=48 * 1024 * 1024
        ),
        cost_estimate=pl.CostEstimate(
            flops=flops, bytes_accessed=8 * 1024 * 1024, transcendentals=tok * every * H
        ),
    )(queries, keys, values, out_grad, branch_ids, node_use)


def solution(mesh):
    rows = P(("group", "dp"), None)
    return jax.shard_map(
        shards,
        mesh=mesh,
        in_specs=(rows, rows, rows, rows, rows, P(("group", "dp"), None, None)),
        out_specs=(rows, rows, rows),
        check_vma=False,
    )
```
